32 devices in a mesh: groups: 2 (over x), tensor: 4 (over y, core), dp: 4 (over z).
Axes of the slice: x: 2, y: 2, z: 4, core: 2. Of those that a mesh axis runs over, the one named last changes fastest.
Arguments:
- gate_pre: bfloat16 [2048, 14336], P(('groups', 'dp'), 'tensor'), parts along dimension 0, may hold values from -6 to 6
- up_pre: bfloat16 [2048, 14336], P(('groups', 'dp'), 'tensor'), parts along dimension 0, may hold values from -6 to 6
- grad_out: bfloat16 [2048, 4096], P(('groups', 'dp', 'tensor')), parts along dimension 0, may hold values from -6 to 6
- down_weight: bfloat16 [14336, 4096], P('tensor'), may hold values from -0.046875 to 0.046875
- delta_values: bfloat16 [64, 128, 128], P(('groups', 'tensor')), parts along dimension 0, may hold values from -0.1796875 to 0.1796875
- delta_rows: int32 [64], P(('groups', 'tensor')), parts along dimension 0, may hold values from 0 to 111, as said below
- delta_cols: int32 [64], P(('groups', 'tensor')), parts along dimension 0, may hold values from 0 to 31
- delta_owner: int32 [64], P(('groups', 'tensor')), parts along dimension 0, may hold values from 0 to 3, as said below
Outputs:
- grad_gate: bfloat16 [2048, 14336], P(('groups', 'dp'), 'tensor'), parts along dimension 0
- grad_up: bfloat16 [2048, 14336], P(('groups', 'dp'), 'tensor'), parts along dimension 0
- delta_grad: float32 [8, 16, 128, 128], P(('groups', 'tensor'), 'dp'), parts along dimension 0
The draws below stay inside these ranges and needn't reach their ends.
There are 2 independent parts, one for each index of `groups`. The reference program is written for one: setup_inputs(seed, part) draws one part's arguments, and reference() takes and returns one part's arrays. A program takes and returns all parts, laid end to end along the dimension named above; an argument that names none is the same for every part. Nothing has to cross between parts.
Inputs may be any that keep to these rules, and one draw needn't show every extreme that they name: Block k lies in the hidden units of tensor shard k // 8: delta_rows[k] // 28 == k // 8. `delta_owner`: among the 8 blocks of one tensor shard at most 4 have one owner, and in every shard some owner has exactly 4.
All inputs are finite; a program needn't handle non-finite values.
Results may differ from the reference program's by a relative error of at most 0.0036.
Values may be sent and summed in bfloat16 or wider, within the bound.
A program may use at most 128 MiB of HBM per device.

```python
import jax
import jax.numpy as jnp
from jax import lax

D = 4096
FF = 14336
BLK = 128
KB = 8
CAP = 4
TOKENS = 1024
NBLK = 32
N_TENSOR = 4
N_DP = 4


def draw_delta_rows(key, part):
    key = jax.random.fold_in(key, 7)
    per_shard = FF // N_TENSOR // BLK
    local_rows = jax.random.randint(key, (N_TENSOR, KB), 0, per_shard)
    shard_start = jnp.arange(N_TENSOR)[:, None] * per_shard
    return (local_rows + shard_start).reshape(-1).astype(jnp.int32)


def draw_delta_owner(key, part):
    key = jax.random.fold_in(key, 11)

    def one_shard(subkey):
        first_key, second_key, third_key = jax.random.split(subkey, 3)
        leading = jax.random.randint(first_key, (), 0, N_DP)
        others = jax.random.randint(second_key, (KB - CAP,), 0, N_DP - 1)
        others = others + (others >= leading).astype(jnp.int32)
        owners = jnp.concatenate([jnp.full((CAP,), leading, jnp.int32), others.astype(jnp.int32)])
        return owners[jax.random.permutation(third_key, KB)]
    return jax.vmap(one_shard)(jax.random.split(key, N_TENSOR)).reshape(-1).astype(jnp.int32)


def with_ends(drawn, key, smallest, largest):
    spot = [jax.random.randint(jax.random.fold_in(key, axis), (), 0, length) for axis, length in enumerate(drawn.shape)]
    widest = drawn.shape.index(max(drawn.shape))
    neighbour = spot[:widest] + [(spot[widest] + 1) % drawn.shape[widest]] + spot[widest + 1:]
    return drawn.at[tuple(spot)].set(smallest).at[tuple(neighbour)].set(largest)


def steps_of(key, shape, cuts, least, top_value):
    factor_of = 1.0
    for axis_at, parts in cuts:
        steps = jax.random.uniform(jax.random.fold_in(jax.random.fold_in(key, 6), axis_at), (parts,), jnp.float32, least / len(cuts), top_value / len(cuts))
        factor_of = factor_of * jnp.repeat(jnp.exp(steps), shape[axis_at] // parts).reshape((-1,) + (1,) * (len(shape) - 1 - axis_at))
    return factor_of


def gaussian(own_key, dims, deviation, bound, shards=(), kind=jnp.bfloat16):
    values = jax.random.normal(own_key, dims, jnp.float32) * deviation
    if len(shards) > 0:
        values = steps_of(own_key, dims, shards, -0.22, 0.18) * values
    return jnp.clip(values, min=-bound, max=bound).astype(kind)


def setup_inputs(seed: int = 0, part: int = 0) -> dict:
    streams_of = jax.random.split(jax.random.key(seed), 9)
    part_splits = jax.random.split(jax.random.fold_in(streams_of[8], part), 9)
    gate_pre = gaussian(part_splits[0], (TOKENS, FF), 1.0, 6.0, ((0, 4), (1, 4)))
    up_pre = gaussian(part_splits[1], (TOKENS, FF), 1.0, 6.0, ((0, 4), (1, 4)))
    grad_out = gaussian(part_splits[2], (TOKENS, D), 1.0, 6.0, ((0, 16),))
    down_weight = gaussian(streams_of[3], (FF, D), FF ** -0.5, 0.046875, ((0, 4),))
    delta_values = gaussian(part_splits[4], (NBLK, BLK, BLK), 0.03, 0.1796875, ((0, 4),))
    delta_rows = draw_delta_rows(jax.random.fold_in(jax.random.fold_in(streams_of[8], part), 71), part)
    delta_cols = with_ends(jax.random.randint(part_splits[6], (NBLK,), 0, D // BLK), jax.random.fold_in(part_splits[6], 1), 0, (D // BLK) - 1).astype(jnp.int32)
    delta_owner = draw_delta_owner(jax.random.fold_in(jax.random.fold_in(streams_of[8], part), 71), part)
    return {"gate_pre": gate_pre, "up_pre": up_pre, "grad_out": grad_out, "down_weight": down_weight, "delta_values": delta_values, "delta_rows": delta_rows, "delta_cols": delta_cols, "delta_owner": delta_owner}


def reference(gate_pre, up_pre, grad_out, down_weight, delta_values, delta_rows, delta_cols, delta_owner):
    gate_val = gate_pre.astype(jnp.float32)
    up_val = up_pre.astype(jnp.float32)
    sigma_val = jax.nn.sigmoid(gate_val)
    active = gate_val * sigma_val
    hidden = (active * up_val).astype(jnp.bfloat16)
    row_blocks = FF // BLK
    col_blocks = D // BLK
    widened = down_weight.astype(jnp.float32).reshape(row_blocks, BLK, col_blocks, BLK)
    widened = widened.at[delta_rows, :, delta_cols, :].add(delta_values.astype(jnp.float32))
    effective = widened.reshape(FF, D).astype(jnp.bfloat16)
    grad_hidden = lax.dot_general(grad_out, effective, (((1,), (1,)), ((), ())), preferred_element_type=jnp.float32)
    grad_gate = (grad_hidden * up_val * sigma_val * (1.0 + gate_val * (1.0 - sigma_val))).astype(jnp.bfloat16)
    grad_up = (grad_hidden * active).astype(jnp.bfloat16)
    hid_blocks = hidden.reshape(TOKENS, row_blocks, BLK)
    out_blocks = grad_out.reshape(TOKENS, col_blocks, BLK)

    def one_block(pair):
        row_index, col_index = pair
        left = hid_blocks[:, row_index, :]
        right = out_blocks[:, col_index, :]
        return jnp.dot(left.T, right, preferred_element_type=jnp.float32)

    block_grad = lax.map(one_block, (delta_rows, delta_cols)) * (TOKENS ** -0.5)
    block_ids = jnp.arange(NBLK).astype(jnp.int32)
    shard_index = (block_ids // KB).astype(jnp.int32)
    earlier = (shard_index[:, None] == shard_index[None, :]) & (delta_owner[:, None] == delta_owner[None, :]) & (block_ids[None, :] < block_ids[:, None])
    rank_index = jnp.sum(earlier.astype(jnp.int32), axis=1).astype(jnp.int32)
    slot_index = (delta_owner * CAP + rank_index).astype(jnp.int32)
    delta_grad = jnp.zeros((N_TENSOR, N_DP * CAP, BLK, BLK), jnp.float32).at[shard_index, slot_index].set(block_grad)
    return grad_gate, grad_up, delta_grad
```

```python
import functools

import jax
import jax.numpy as jnp
from jax import lax
from jax.experimental import pallas as pl
from jax.experimental.pallas import tpu as pltpu
from jax.sharding import PartitionSpec as P

CAP = 4
CORES = 2
MESH = pl.DeviceIdType.MESH
F32 = jnp.float32
BF16 = jnp.bfloat16
NT = (((1,), (1,)), ((), ()))


def widest(total, options):
    for option in options:
        if total % option == 0:
            return option
    return total


def kernel(
    n_t, n_d, rows_ref, cols_ref, owner_ref, gate_hbm, up_hbm, go_hbm, w_hbm, dv_ref,
    gg_hbm, gu_hbm, dg_hbm,
    gate_v, up_v, slope_v, act_v, go_v, w_v, acc_v, all_hid_v, go_col_v, hid_v, term_v, send_v, recv_v, corr_v, comb_v, own_v,
    in_sem, w_sem, out_sem, dg_sem, sib_sem, cs_sem, cr_sem, fs_sem, fr_sem, rs_sem, rr_sem,
):
    tok, ff = gate_v.shape
    depth = w_v.shape[1]
    shard_tok = go_hbm.shape[0]
    blocks, side = dv_ref.shape[0], dv_ref.shape[1]
    n_y = n_t // CORES
    chunks = w_sem.shape[0]
    wide = depth // chunks
    tile = widest(ff, (512, 256, 128))
    tiles = ff // tile
    me_t = lax.axis_index("tensor")
    me_d = lax.axis_index("dp")
    core = lax.rem(me_t, CORES)
    me_y = lax.div(me_t, CORES)
    sibling = me_y * CORES + (1 - core)

    def on_y(offset):
        return lax.rem(me_y + offset + n_y, n_y) * CORES + core

    def tokens_of(t):
        return pl.ds(pl.multiple_of(t * shard_tok, shard_tok), shard_tok)

    gate_in = pltpu.make_async_copy(gate_hbm, gate_v, in_sem.at[0])
    up_in = pltpu.make_async_copy(up_hbm, up_v, in_sem.at[1])
    go_in = pltpu.make_async_copy(go_hbm, go_v.at[tokens_of(me_t)], in_sem.at[2])
    gate_in.start()
    up_in.start()
    go_in.start()
    w_in = []
    for c in range(chunks):
        span = pl.ds(c * wide, wide)
        w_in.append(pltpu.make_async_copy(w_hbm.at[:, span], w_v.at[:, span], w_sem.at[c]))
        w_in[-1].start()

    barrier = pltpu.get_barrier_semaphore()
    pl.semaphore_signal(barrier, inc=1, device_id={"tensor": sibling}, device_id_type=MESH)
    for off in range(1, n_y):
        pl.semaphore_signal(barrier, inc=1, device_id={"tensor": on_y(off)}, device_id_type=MESH)
    for off in range(1, n_d):
        peer = lax.rem(me_d + off, n_d)
        pl.semaphore_signal(barrier, inc=1, device_id={"dp": peer}, device_id_type=MESH)
    pl.semaphore_wait(barrier, 1 + (n_y - 1) + (n_d - 1))

    cross, forward = {}, {}
    for c in range(chunks):
        span = pl.ds(c * wide, wide)
        for off in range(1, n_y):
            cross[off, c] = pltpu.make_async_remote_copy(
                src_ref=go_hbm.at[:, span], dst_ref=go_v.at[tokens_of(me_t), span],
                send_sem=cs_sem.at[off - 1, c], recv_sem=cr_sem.at[off - 1, c],
                device_id={"tensor": on_y(off)}, device_id_type=MESH)
            cross[off, c].start()
    to_sibling = pltpu.make_async_remote_copy(
        src_ref=go_hbm, dst_ref=go_v.at[tokens_of(me_t)],
        send_sem=sib_sem.at[0], recv_sem=sib_sem.at[1],
        device_id={"tensor": sibling}, device_id_type=MESH)
    to_sibling.start()

    gate_in.wait()
    up_in.wait()
    strip = 64
    strips = tok // strip

    def factors(step, carry):
        rows = pl.ds(pl.multiple_of(lax.rem(step, strips) * strip, strip), strip)
        span = pl.ds(pl.multiple_of(lax.div(step, strips) * side, side), side)
        gate = gate_v[rows, span].astype(F32)
        sigma = jax.nn.sigmoid(gate)
        act = gate * sigma
        up = up_v[rows, span].astype(F32)
        act_v[rows, span] = act
        slope_v[rows, span] = up * (sigma * (1.0 + gate * (1.0 - sigma)))
        all_hid_v[lax.div(step, strips), rows] = (act * up).astype(BF16)
        return carry

    lax.fori_loop(0, strips * (ff // side), factors, 0, unroll=2)

    row = [lax.rem(rows_ref[k], ff // side) for k in range(blocks)]
    col = [cols_ref[k] for k in range(blocks)]
    owner = [owner_ref[k] for k in range(blocks)]
    slot = []
    for k in range(blocks):
        rank = jnp.int32(0)
        for k2 in range(k):
            rank = rank + (owner[k2] == owner[k]).astype(jnp.int32)
        slot.append(owner[k] * CAP + rank)

    first = []
    for k in range(blocks):
        alone = jnp.int32(1)
        for k2 in range(k):
            alone = alone * (1 - (row[k2] == row[k]).astype(jnp.int32))
        first.append(alone)

    def block_in(s):
        found = jnp.int32(blocks)
        for k in range(blocks):
            found = found + (slot[k] == s).astype(jnp.int32) * (k - blocks)
        return found

    for k in range(blocks):
        hid_v[k] = all_hid_v[row[k]].astype(F32).T.astype(BF16)

    def partial_sum(c, j):
        span = pl.ds(c * wide, wide)
        part = pl.ds(pl.multiple_of(j * tile, tile), tile)
        return lax.dot_general(go_v[:, span], w_v[part, span], NT, preferred_element_type=F32)

    def by_column(c):
        for i in range(c * wide // side, (c + 1) * wide // side):
            go_col_v[i] = go_v[:, i * side:(i + 1) * side]

    def chunk_step(c):
        by_column(c)
        w_in[c].wait()

        def body(j, carry):
            part = pl.ds(pl.multiple_of(j * tile, tile), tile)
            got = partial_sum(c, j)
            if c == 0:
                acc_v[:, part] = got
            else:
                acc_v[:, part] = acc_v[:, part] + got
            return carry

        lax.fori_loop(0, tiles, body, 0)

    for c in range(chunks):
        span = pl.ds(c * wide, wide)
        for off in range(1, n_y):
            cross[off, c].wait_recv()
            source = on_y(-off)
            forward[off, c] = pltpu.make_async_remote_copy(
                src_ref=go_v.at[tokens_of(source), span], dst_ref=go_v.at[tokens_of(source), span],
                send_sem=fs_sem.at[off - 1, c], recv_sem=fr_sem.at[off - 1, c],
                device_id={"tensor": sibling}, device_id_type=MESH)
            forward[off, c].start()
        if c == 0:
            go_in.wait()
            to_sibling.wait_recv()
        else:
            for off in range(1, n_y):
                forward[off, c - 1].wait_recv()
            chunk_step(c - 1)
    for off in range(1, n_y):
        forward[off, chunks - 1].wait_recv()
    by_column(chunks - 1)

    scale = float(tok * n_d) ** -0.5
    for k in range(blocks):
        term_v[k] = scale * jnp.dot(hid_v[k], go_col_v[col[k]], preferred_element_type=F32)
    term_v[blocks] = jnp.zeros((side, side), F32)
    for s in range(n_d * CAP):
        send_v[s] = term_v[block_in(s)].astype(BF16)
    scatter = []
    for off in range(1, n_d):
        peer = lax.rem(me_d + off, n_d)
        scatter.append(pltpu.make_async_remote_copy(
            src_ref=send_v.at[pl.ds(peer * CAP, CAP)], dst_ref=recv_v.at[off - 1],
            send_sem=rs_sem.at[off - 1], recv_sem=rr_sem.at[off - 1],
            device_id={"dp": peer}, device_id_type=MESH))
        scatter[-1].start()

    for k in range(blocks):
        corr_v[k] = lax.dot_general(go_col_v[col[k]], dv_ref[k], NT, preferred_element_type=F32)
    for k in range(blocks):
        total = corr_v[k]
        for k2 in range(blocks):
            if k2 != k:
                total = total + (row[k2] == row[k]).astype(jnp.int32).astype(F32) * corr_v[k2]
        comb_v[k] = total
    comb_v[blocks] = jnp.zeros((tok, side), F32)

    def outputs(j):
        part = pl.ds(pl.multiple_of(j * tile, tile), tile)
        return (pltpu.make_async_copy(gate_v.at[:, part], gg_hbm.at[:, part], out_sem.at[0, j]),
                pltpu.make_async_copy(up_v.at[:, part], gu_hbm.at[:, part], out_sem.at[1, j]))

    w_in[chunks - 1].wait()

    def last(j, carry):
        got = partial_sum(chunks - 1, j)
        for i in range(tile // side):
            part = pl.ds(pl.multiple_of(j * tile + i * side, side), side)
            which = j * (tile // side) + i
            found = jnp.int32(blocks)
            for k in range(blocks):
                found = found + first[k] * (row[k] == which).astype(jnp.int32) * (k - blocks)
            grad = got[:, i * side:(i + 1) * side] + acc_v[:, part] + comb_v[found]
            gate_v[:, part] = (grad * slope_v[:, part]).astype(BF16)
            up_v[:, part] = (grad * act_v[:, part]).astype(BF16)
        for copy in outputs(j):
            copy.start()
        return carry

    lax.fori_loop(0, tiles, last, 0)

    for i in range(CAP):
        own_v[0, i] = term_v[block_in(me_d * CAP + i)]
    for off in range(1, n_d):
        scatter[off - 1].wait_recv()
    for i in range(CAP):
        total = own_v[0, i]
        for off in range(1, n_d):
            total = total + recv_v[off - 1, i].astype(F32)
        own_v[0, i] = total
    dg_out = pltpu.make_async_copy(own_v, dg_hbm, dg_sem)
    dg_out.start()

    def drain(j, carry):
        for copy in outputs(j):
            copy.wait()
        return carry

    lax.fori_loop(0, tiles, drain, 0)
    for c in range(chunks):
        for off in range(1, n_y):
            cross[off, c].wait_send()
            forward[off, c].wait_send()
    to_sibling.wait_send()
    for copy in scatter:
        copy.wait_send()
    dg_out.wait()


def local(n_t, n_d, gate_pre, up_pre, grad_out, down_weight, delta_values, delta_rows, delta_cols, delta_owner):
    tok, ff = gate_pre.shape
    depth = down_weight.shape[1]
    blocks, side = delta_values.shape[0], delta_values.shape[1]
    chunks = 4
    n_y = n_t // CORES
    tiles = ff // widest(ff, (512, 256, 128))
    smem = pl.BlockSpec(memory_space=pltpu.SMEM)
    anywhere = pl.BlockSpec(memory_space=pl.ANY)
    vmem = pl.BlockSpec(memory_space=pltpu.VMEM)
    dma = pltpu.SemaphoreType.DMA
    return pl.pallas_call(
        functools.partial(kernel, n_t, n_d),
        out_shape=(
            jax.ShapeDtypeStruct((tok, ff), BF16),
            jax.ShapeDtypeStruct((tok, ff), BF16),
            jax.ShapeDtypeStruct((1, CAP, side, side), F32),
        ),
        in_specs=[smem] * 3 + [anywhere] * 4 + [vmem],
        out_specs=(anywhere, anywhere, anywhere),
        scratch_shapes=[
            pltpu.VMEM((tok, ff), BF16),
            pltpu.VMEM((tok, ff), BF16),
            pltpu.VMEM((tok, ff), F32),
            pltpu.VMEM((tok, ff), F32),
            pltpu.VMEM((tok, depth), BF16),
            pltpu.VMEM((ff, depth), BF16),
            pltpu.VMEM((tok, ff), F32),
            pltpu.VMEM((ff // side, tok, side), BF16),
            pltpu.VMEM((depth // side, tok, side), BF16),
            pltpu.VMEM((blocks, side, tok), BF16),
            pltpu.VMEM((blocks + 1, side, side), F32),
            pltpu.VMEM((n_d * CAP, side, side), BF16),
            pltpu.VMEM((n_d - 1, CAP, side, side), BF16),
            pltpu.VMEM((blocks, tok, side), F32),
            pltpu.VMEM((blocks + 1, tok, side), F32),
            pltpu.VMEM((1, CAP, side, side), F32),
            dma((3,)),
            dma((chunks,)),
            dma((2, tiles)),
            dma,
            dma((2,)),
            dma((n_y - 1, chunks)),
            dma((n_y - 1, chunks)),
            dma((n_y - 1, chunks)),
            dma((n_y - 1, chunks)),
            dma((n_d - 1,)),
            dma((n_d - 1,)),
        ],
        compiler_params=pltpu.CompilerParams(
            collective_id=0, has_side_effects=True, vmem_limit_bytes=60 * 2**20
        ),
    )(delta_rows, delta_cols, delta_owner, gate_pre, up_pre, grad_out, down_weight, delta_values)


def solution(mesh):
    placed = (
        P(("groups", "dp"), "tensor"),
        P(("groups", "dp"), "tensor"),
        P(("groups", "dp", "tensor"), None),
        P("tensor", None),
        P(("groups", "tensor"), None, None),
        P(("groups", "tensor")),
        P(("groups", "tensor")),
        P(("groups", "tensor")),
    )
    return jax.shard_map(
        functools.partial(local, mesh.shape["tensor"], mesh.shape["dp"]),
        mesh=mesh,
        in_specs=placed,
        out_specs=(
            P(("groups", "dp"), "tensor"),
            P(("groups", "dp"), "tensor"),
            P(("groups", "tensor"), "dp", None, None),
        ),
        check_vma=False,
    )
```

```python
import functools

import jax
import jax.numpy as jnp
from jax import lax
from jax.experimental import pallas as pl
from jax.experimental.pallas import tpu as pltpu
from jax.sharding import PartitionSpec as P

CAP = 4
CORES = 2
TILES = (1792, 896, 512, 256, 128)
MESH = pl.DeviceIdType.MESH
F32 = jnp.float32
BF16 = jnp.bfloat16
NT = (((1,), (1,)), ((), ()))


def widest(total, options):
    for option in options:
        if total % option == 0:
            return option
    return total


def kernel(
    n_t, n_d, rows_ref, cols_ref, owner_ref, gate_hbm, up_hbm, go_hbm, w_hbm, dv_ref,
    gg_hbm, gu_hbm, dg_hbm,
    gate_v, up_v, slope_v, act_v, go_v, w_v, acc_v, all_hid_v, go_col_v, hid_v, term_v, send_v, recv_v, mix_v, comb_v, own_v,
    in_sem, w_sem, out_sem, dg_sem, sib_sem, cs_sem, cr_sem, fs_sem, fr_sem, rs_sem, rr_sem,
):
    tok, ff = gate_v.shape
    depth = w_v.shape[1]
    shard_tok = go_hbm.shape[0]
    blocks, side = dv_ref.shape[0], dv_ref.shape[1]
    n_y = n_t // CORES
    chunks = w_sem.shape[0]
    wide = depth // chunks
    tile = widest(ff, TILES)
    tiles = ff // tile
    me_t = lax.axis_index("tensor")
    me_d = lax.axis_index("dp")
    core = lax.rem(me_t, CORES)
    me_y = lax.div(me_t, CORES)
    sibling = me_y * CORES + (1 - core)

    def on_y(offset):
        return lax.rem(me_y + offset + n_y, n_y) * CORES + core

    def tokens_of(t):
        return pl.ds(pl.multiple_of(t * shard_tok, shard_tok), shard_tok)

    gate_in = pltpu.make_async_copy(gate_hbm, gate_v, in_sem.at[0])
    up_in = pltpu.make_async_copy(up_hbm, up_v, in_sem.at[1])
    go_in = pltpu.make_async_copy(go_hbm, go_v.at[tokens_of(me_t)], in_sem.at[2])
    gate_in.start()
    up_in.start()
    go_in.start()
    w_in = []
    for c in range(chunks):
        span = pl.ds(c * wide, wide)
        w_in.append(pltpu.make_async_copy(w_hbm.at[:, span], w_v.at[:, span], w_sem.at[c]))
        w_in[-1].start()

    barrier = pltpu.get_barrier_semaphore()
    pl.semaphore_signal(barrier, inc=1, device_id={"tensor": sibling}, device_id_type=MESH)
    for off in range(1, n_y):
        pl.semaphore_signal(barrier, inc=1, device_id={"tensor": on_y(off)}, device_id_type=MESH)
    for off in range(1, n_d):
        peer = lax.rem(me_d + off, n_d)
        pl.semaphore_signal(barrier, inc=1, device_id={"dp": peer}, device_id_type=MESH)
    pl.semaphore_wait(barrier, 1 + (n_y - 1) + (n_d - 1))

    cross, forward = {}, {}
    early = chunks - 2
    for c in range(chunks):
        span = pl.ds(c * wide, wide)
        for off in range(1, n_y):
            cross[off, c] = pltpu.make_async_remote_copy(
                src_ref=go_hbm.at[:, span], dst_ref=go_v.at[tokens_of(me_t), span],
                send_sem=cs_sem.at[off - 1, c], recv_sem=cr_sem.at[off - 1, c],
                device_id={"tensor": on_y(off)}, device_id_type=MESH)
            cross[off, c].start()
    to_sibling = pltpu.make_async_remote_copy(
        src_ref=go_hbm, dst_ref=go_v.at[tokens_of(me_t)],
        send_sem=sib_sem.at[0], recv_sem=sib_sem.at[1],
        device_id={"tensor": sibling}, device_id_type=MESH)
    to_sibling.start()

    gate_in.wait()
    up_in.wait()
    strip = tok
    strips = tok // strip

    def factors(step, carry):
        rows = pl.ds(pl.multiple_of(lax.rem(step, strips) * strip, strip), strip)
        span = pl.ds(pl.multiple_of(lax.div(step, strips) * side, side), side)
        gate = gate_v[rows, span].astype(F32)
        sigma = jax.nn.sigmoid(gate)
        act = gate * sigma
        up = up_v[rows, span].astype(F32)
        act_v[rows, span] = act
        slope_v[rows, span] = up * (sigma * (1.0 + gate * (1.0 - sigma)))
        all_hid_v[lax.div(step, strips), rows] = (act * up).astype(BF16)
        return carry

    lax.fori_loop(0, strips * (ff // side), factors, 0)

    row = [lax.rem(rows_ref[k], ff // side) for k in range(blocks)]
    col = [cols_ref[k] for k in range(blocks)]
    owner = [owner_ref[k] for k in range(blocks)]
    slot = []
    for k in range(blocks):
        rank = jnp.int32(0)
        for k2 in range(k):
            rank = rank + (owner[k2] == owner[k]).astype(jnp.int32)
        slot.append(owner[k] * CAP + rank)

    first = []
    for k in range(blocks):
        alone = jnp.int32(1)
        for k2 in range(k):
            alone = alone * (1 - (row[k2] == row[k]).astype(jnp.int32))
        first.append(alone)

    def block_in(s):
        found = jnp.int32(blocks)
        for k in range(blocks):
            found = found + (slot[k] == s).astype(jnp.int32) * (k - blocks)
        return found

    for k in range(blocks):
        hid_v[k] = all_hid_v[row[k]].astype(F32).T.astype(BF16)

    for k in range(blocks):
        for k2 in range(blocks):
            spot = (slice(k * side, (k + 1) * side), slice(k2 * side, (k2 + 1) * side))
            if k2 == k:
                mix_v[spot] = dv_ref[k2]
            else:
                same = (row[k2] == row[k]).astype(jnp.int32).astype(F32)
                mix_v[spot] = (same * dv_ref[k2].astype(F32)).astype(BF16)

    def partial_sum(c, count, j):
        span = pl.ds(c * wide, count * wide)
        part = pl.ds(pl.multiple_of(j * tile, tile), tile)
        return lax.dot_general(go_v[:, span], w_v[part, span], NT, preferred_element_type=F32)

    def by_column(c):
        for i in range(c * wide // side, (c + 1) * wide // side):
            go_col_v[i] = go_v[:, i * side:(i + 1) * side]

    def chunk_step(c):
        w_in[c].wait()

        def body(j, carry):
            part = pl.ds(pl.multiple_of(j * tile, tile), tile)
            got = partial_sum(c, 1, j)
            if c == 0:
                acc_v[:, part] = got
            else:
                acc_v[:, part] = acc_v[:, part] + got
            return carry

        lax.fori_loop(0, tiles, body, 0)

    for c in range(chunks):
        span = pl.ds(c * wide, wide)
        for off in range(1, n_y):
            cross[off, c].wait_recv()
            source = on_y(-off)
            forward[off, c] = pltpu.make_async_remote_copy(
                src_ref=go_v.at[tokens_of(source), span], dst_ref=go_v.at[tokens_of(source), span],
                send_sem=fs_sem.at[off - 1, c], recv_sem=fr_sem.at[off - 1, c],
                device_id={"tensor": sibling}, device_id_type=MESH)
            forward[off, c].start()
        if c == 0:
            go_in.wait()
            to_sibling.wait_recv()
        else:
            for off in range(1, n_y):
                forward[off, c - 1].wait_recv()
            by_column(c - 1)
            if c - 1 < early:
                chunk_step(c - 1)
    for off in range(1, n_y):
        forward[off, chunks - 1].wait_recv()
    by_column(chunks - 1)

    scale = float(tok * n_d) ** -0.5
    for k in range(blocks):
        term_v[k] = scale * jnp.dot(hid_v[k], go_col_v[col[k]], preferred_element_type=F32)
    term_v[blocks] = jnp.zeros((side, side), F32)
    for s in range(n_d * CAP):
        send_v[s] = term_v[block_in(s)].astype(BF16)
    scatter = []
    for off in range(1, n_d):
        peer = lax.rem(me_d + off, n_d)
        scatter.append(pltpu.make_async_remote_copy(
            src_ref=send_v.at[pl.ds(peer * CAP, CAP)], dst_ref=recv_v.at[off - 1],
            send_sem=rs_sem.at[off - 1], recv_sem=rr_sem.at[off - 1],
            device_id={"dp": peer}, device_id_type=MESH))
        scatter[-1].start()

    picked = jnp.concatenate([go_col_v[col[k]] for k in range(blocks)], axis=1)
    added = lax.dot_general(picked, mix_v[...], NT, preferred_element_type=F32)
    for k in range(blocks):
        comb_v[k] = added[:, k * side:(k + 1) * side]
    comb_v[blocks] = jnp.zeros((tok, side), F32)

    def outputs(j):
        part = pl.ds(pl.multiple_of(j * tile, tile), tile)
        return (pltpu.make_async_copy(gate_v.at[:, part], gg_hbm.at[:, part], out_sem.at[0, j]),
                pltpu.make_async_copy(up_v.at[:, part], gu_hbm.at[:, part], out_sem.at[1, j]))

    for c in range(early, chunks):
        w_in[c].wait()

    def last(j, carry):
        got = partial_sum(early, chunks - early, j)
        for i in range(tile // side):
            part = pl.ds(pl.multiple_of(j * tile + i * side, side), side)
            which = j * (tile // side) + i
            found = jnp.int32(blocks)
            for k in range(blocks):
                found = found + first[k] * (row[k] == which).astype(jnp.int32) * (k - blocks)
            grad = got[:, i * side:(i + 1) * side] + acc_v[:, part] + comb_v[found]
            gate_v[:, part] = (grad * slope_v[:, part]).astype(BF16)
            up_v[:, part] = (grad * act_v[:, part]).astype(BF16)
        for copy in outputs(j):
            copy.start()
        return carry

    lax.fori_loop(0, tiles, last, 0)

    for i in range(CAP):
        own_v[0, i] = term_v[block_in(me_d * CAP + i)]
    for off in range(1, n_d):
        scatter[off - 1].wait_recv()
    for i in range(CAP):
        total = own_v[0, i]
        for off in range(1, n_d):
            total = total + recv_v[off - 1, i].astype(F32)
        own_v[0, i] = total
    dg_out = pltpu.make_async_copy(own_v, dg_hbm, dg_sem)
    dg_out.start()

    def drain(j, carry):
        for copy in outputs(j):
            copy.wait()
        return carry

    lax.fori_loop(0, tiles, drain, 0)
    for c in range(chunks):
        for off in range(1, n_y):
            cross[off, c].wait_send()
            forward[off, c].wait_send()
    to_sibling.wait_send()
    for copy in scatter:
        copy.wait_send()
    dg_out.wait()


def local(n_t, n_d, gate_pre, up_pre, grad_out, down_weight, delta_values, delta_rows, delta_cols, delta_owner):
    tok, ff = gate_pre.shape
    depth = down_weight.shape[1]
    blocks, side = delta_values.shape[0], delta_values.shape[1]
    chunks = 4
    n_y = n_t // CORES
    tiles = ff // widest(ff, TILES)
    smem = pl.BlockSpec(memory_space=pltpu.SMEM)
    anywhere = pl.BlockSpec(memory_space=pl.ANY)
    vmem = pl.BlockSpec(memory_space=pltpu.VMEM)
    dma = pltpu.SemaphoreType.DMA
    return pl.pallas_call(
        functools.partial(kernel, n_t, n_d),
        out_shape=(
            jax.ShapeDtypeStruct((tok, ff), BF16),
            jax.ShapeDtypeStruct((tok, ff), BF16),
            jax.ShapeDtypeStruct((1, CAP, side, side), F32),
        ),
        in_specs=[smem] * 3 + [anywhere] * 4 + [vmem],
        out_specs=(anywhere, anywhere, anywhere),
        scratch_shapes=[
            pltpu.VMEM((tok, ff), BF16),
            pltpu.VMEM((tok, ff), BF16),
            pltpu.VMEM((tok, ff), F32),
            pltpu.VMEM((tok, ff), F32),
            pltpu.VMEM((tok, depth), BF16),
            pltpu.VMEM((ff, depth), BF16),
            pltpu.VMEM((tok, ff), F32),
            pltpu.VMEM((ff // side, tok, side), BF16),
            pltpu.VMEM((depth // side, tok, side), BF16),
            pltpu.VMEM((blocks, side, tok), BF16),
            pltpu.VMEM((blocks + 1, side, side), F32),
            pltpu.VMEM((n_d * CAP, side, side), BF16),
            pltpu.VMEM((n_d - 1, CAP, side, side), BF16),
            pltpu.VMEM((blocks * side, blocks * side), BF16),
            pltpu.VMEM((blocks + 1, tok, side), F32),
            pltpu.VMEM((1, CAP, side, side), F32),
            dma((3,)),
            dma((chunks,)),
            dma((2, tiles)),
            dma,
            dma((2,)),
            dma((n_y - 1, chunks)),
            dma((n_y - 1, chunks)),
            dma((n_y - 1, chunks)),
            dma((n_y - 1, chunks)),
            dma((n_d - 1,)),
            dma((n_d - 1,)),
        ],
        compiler_params=pltpu.CompilerParams(
            collective_id=0, has_side_effects=True, vmem_limit_bytes=56 * 2**20
        ),
    )(delta_rows, delta_cols, delta_owner, gate_pre, up_pre, grad_out, down_weight, delta_values)


def solution(mesh):
    placed = (
        P(("groups", "dp"), "tensor"),
        P(("groups", "dp"), "tensor"),
        P(("groups", "dp", "tensor"), None),
        P("tensor", None),
        P(("groups", "tensor"), None, None),
        P(("groups", "tensor")),
        P(("groups", "tensor")),
        P(("groups", "tensor")),
    )
    return jax.shard_map(
        functools.partial(local, mesh.shape["tensor"], mesh.shape["dp"]),
        mesh=mesh,
        in_specs=placed,
        out_specs=(
            P(("groups", "dp"), "tensor"),
            P(("groups", "dp"), "tensor"),
            P(("groups", "tensor"), "dp", None, None),
        ),
        check_vma=False,
    )
```

```python
import functools

import jax
import jax.numpy as jnp
from jax import lax
from jax.experimental import pallas as pl
from jax.experimental.pallas import tpu as pltpu
from jax.sharding import PartitionSpec as P

CAP = 4
CORES = 2
TILES = (1792, 896, 512, 256, 128)
MESH = pl.DeviceIdType.MESH
F32 = jnp.float32
BF16 = jnp.bfloat16
NT = (((1,), (1,)), ((), ()))


def widest(total, options):
    for option in options:
        if total % option == 0:
            return option
    return total


def kernel(
    n_t, n_d, rows_ref, cols_ref, owner_ref, gate_hbm, up_hbm, go_hbm, w_hbm, dv_ref,
    gg_hbm, gu_hbm, dg_hbm,
    gate_v, up_v, slope_v, act_v, go_v, w_v, acc_v, all_hid_v, go_col_v, hid_v, term_v, send_v, recv_v, mix_v, comb_v, own_v,
    in_sem, w_sem, out_sem, dg_sem, sib_sem, cs_sem, cr_sem, fs_sem, fr_sem, rs_sem, rr_sem,
):
    tok, ff = gate_v.shape
    depth = w_v.shape[1]
    shard_tok = go_hbm.shape[0]
    blocks, side = dv_ref.shape[0], dv_ref.shape[1]
    n_y = n_t // CORES
    chunks = w_sem.shape[0]
    wide = depth // chunks
    tile = widest(ff, TILES)
    tiles = ff // tile
    me_t = lax.axis_index("tensor")
    me_d = lax.axis_index("dp")
    core = lax.rem(me_t, CORES)
    me_y = lax.div(me_t, CORES)
    sibling = me_y * CORES + (1 - core)

    def on_y(offset):
        return lax.rem(me_y + offset + n_y, n_y) * CORES + core

    def tokens_of(t):
        return pl.ds(pl.multiple_of(t * shard_tok, shard_tok), shard_tok)

    gate_in = pltpu.make_async_copy(gate_hbm, gate_v, in_sem.at[0])
    up_in = pltpu.make_async_copy(up_hbm, up_v, in_sem.at[1])
    go_in = pltpu.make_async_copy(go_hbm, go_v.at[tokens_of(me_t)], in_sem.at[2])
    gate_in.start()
    up_in.start()
    go_in.start()
    w_in = []
    for c in range(chunks):
        span = pl.ds(c * wide, wide)
        w_in.append(pltpu.make_async_copy(w_hbm.at[:, span], w_v.at[:, span], w_sem.at[c]))

    barrier = pltpu.get_barrier_semaphore()
    pl.semaphore_signal(barrier, inc=1, device_id={"tensor": sibling}, device_id_type=MESH)
    for off in range(1, n_y):
        pl.semaphore_signal(barrier, inc=1, device_id={"tensor": on_y(off)}, device_id_type=MESH)
    for off in range(1, n_d):
        peer = lax.rem(me_d + off, n_d)
        pl.semaphore_signal(barrier, inc=1, device_id={"dp": peer}, device_id_type=MESH)
    pl.semaphore_wait(barrier, 1 + (n_y - 1) + (n_d - 1))

    cross, forward = {}, {}
    early = chunks - 2
    for c in range(chunks):
        span = pl.ds(c * wide, wide)
        for off in range(1, n_y):
            cross[off, c] = pltpu.make_async_remote_copy(
                src_ref=go_hbm.at[:, span], dst_ref=go_v.at[tokens_of(me_t), span],
                send_sem=cs_sem.at[off - 1, c], recv_sem=cr_sem.at[off - 1, c],
                device_id={"tensor": on_y(off)}, device_id_type=MESH)
            cross[off, c].start()
    to_sibling = pltpu.make_async_remote_copy(
        src_ref=go_hbm, dst_ref=go_v.at[tokens_of(me_t)],
        send_sem=sib_sem.at[0], recv_sem=sib_sem.at[1],
        device_id={"tensor": sibling}, device_id_type=MESH)
    to_sibling.start()
    for copy in w_in:
        copy.start()

    gate_in.wait()
    up_in.wait()
    strip = tok
    strips = tok // strip

    def factors(step, carry):
        rows = pl.ds(pl.multiple_of(lax.rem(step, strips) * strip, strip), strip)
        span = pl.ds(pl.multiple_of(lax.div(step, strips) * side, side), side)
        gate = gate_v[rows, span].astype(F32)
        sigma = jax.nn.sigmoid(gate)
        act = gate * sigma
        up = up_v[rows, span].astype(F32)
        act_v[rows, span] = act
        slope_v[rows, span] = up * (sigma * (1.0 + gate * (1.0 - sigma)))
        all_hid_v[lax.div(step, strips), rows] = (act * up).astype(BF16)
        return carry

    lax.fori_loop(0, strips * (ff // side), factors, 0)

    row = [lax.rem(rows_ref[k], ff // side) for k in range(blocks)]
    col = [cols_ref[k] for k in range(blocks)]
    owner = [owner_ref[k] for k in range(blocks)]
    slot = []
    for k in range(blocks):
        rank = jnp.int32(0)
        for k2 in range(k):
            rank = rank + (owner[k2] == owner[k]).astype(jnp.int32)
        slot.append(owner[k] * CAP + rank)

    first = []
    for k in range(blocks):
        alone = jnp.int32(1)
        for k2 in range(k):
            alone = alone * (1 - (row[k2] == row[k]).astype(jnp.int32))
        first.append(alone)

    def block_in(s):
        found = jnp.int32(blocks)
        for k in range(blocks):
            found = found + (slot[k] == s).astype(jnp.int32) * (k - blocks)
        return found

    for k in range(blocks):
        hid_v[k] = all_hid_v[row[k]].astype(F32).T.astype(BF16)

    for k in range(blocks):
        for k2 in range(blocks):
            spot = (slice(k * side, (k + 1) * side), slice(k2 * side, (k2 + 1) * side))
            if k2 == k:
                mix_v[spot] = dv_ref[k2]
            else:
                same = (row[k2] == row[k]).astype(jnp.int32).astype(F32)
                mix_v[spot] = (same * dv_ref[k2].astype(F32)).astype(BF16)

    def partial_sum(c, count, j):
        span = pl.ds(c * wide, count * wide)
        part = pl.ds(pl.multiple_of(j * tile, tile), tile)
        return lax.dot_general(go_v[:, span], w_v[part, span], NT, preferred_element_type=F32)

    def by_column(c):
        for i in range(c * wide // side, (c + 1) * wide // side):
            go_col_v[i] = go_v[:, i * side:(i + 1) * side]

    def chunk_step(c):
        w_in[c].wait()

        def body(j, carry):
            part = pl.ds(pl.multiple_of(j * tile, tile), tile)
            got = partial_sum(c, 1, j)
            if c == 0:
                acc_v[:, part] = got
            else:
                acc_v[:, part] = acc_v[:, part] + got
            return carry

        lax.fori_loop(0, tiles, body, 0)

    for c in range(chunks):
        span = pl.ds(c * wide, wide)
        for off in range(1, n_y):
            cross[off, c].wait_recv()
            source = on_y(-off)
            forward[off, c] = pltpu.make_async_remote_copy(
                src_ref=go_v.at[tokens_of(source), span], dst_ref=go_v.at[tokens_of(source), span],
                send_sem=fs_sem.at[off - 1, c], recv_sem=fr_sem.at[off - 1, c],
                device_id={"tensor": sibling}, device_id_type=MESH)
            forward[off, c].start()
        if c == 0:
            go_in.wait()
            to_sibling.wait_recv()
        else:
            for off in range(1, n_y):
                forward[off, c - 1].wait_recv()
            by_column(c - 1)
            if c - 1 < early:
                chunk_step(c - 1)
    for off in range(1, n_y):
        forward[off, chunks - 1].wait_recv()
    by_column(chunks - 1)

    scale = float(tok * n_d) ** -0.5
    for k in range(blocks):
        term_v[k] = scale * jnp.dot(hid_v[k], go_col_v[col[k]], preferred_element_type=F32)
    term_v[blocks] = jnp.zeros((side, side), F32)
    for s in range(n_d * CAP):
        send_v[s] = term_v[block_in(s)].astype(BF16)
    scatter = []
    for off in range(1, n_d):
        peer = lax.rem(me_d + off, n_d)
        scatter.append(pltpu.make_async_remote_copy(
            src_ref=send_v.at[pl.ds(peer * CAP, CAP)], dst_ref=recv_v.at[off - 1],
            send_sem=rs_sem.at[off - 1], recv_sem=rr_sem.at[off - 1],
            device_id={"dp": peer}, device_id_type=MESH))
        scatter[-1].start()

    picked = jnp.concatenate([go_col_v[col[k]] for k in range(blocks)], axis=1)
    added = lax.dot_general(picked, mix_v[...], NT, preferred_element_type=F32)
    for k in range(blocks):
        comb_v[k] = added[:, k * side:(k + 1) * side]
    comb_v[blocks] = jnp.zeros((tok, side), F32)

    def outputs(j):
        part = pl.ds(pl.multiple_of(j * tile, tile), tile)
        return (pltpu.make_async_copy(gate_v.at[:, part], gg_hbm.at[:, part], out_sem.at[0, j]),
                pltpu.make_async_copy(up_v.at[:, part], gu_hbm.at[:, part], out_sem.at[1, j]))

    for c in range(early, chunks):
        w_in[c].wait()

    def last(j, carry):
        got = partial_sum(early, chunks - early, j)
        for i in range(tile // side):
            part = pl.ds(pl.multiple_of(j * tile + i * side, side), side)
            which = j * (tile // side) + i
            found = jnp.int32(blocks)
            for k in range(blocks):
                found = found + first[k] * (row[k] == which).astype(jnp.int32) * (k - blocks)
            grad = got[:, i * side:(i + 1) * side] + acc_v[:, part] + comb_v[found]
            gate_v[:, part] = (grad * slope_v[:, part]).astype(BF16)
            up_v[:, part] = (grad * act_v[:, part]).astype(BF16)
        for copy in outputs(j):
            copy.start()
        return carry

    lax.fori_loop(0, tiles, last, 0)

    for i in range(CAP):
        own_v[0, i] = term_v[block_in(me_d * CAP + i)]
    for off in range(1, n_d):
        scatter[off - 1].wait_recv()
    for i in range(CAP):
        total = own_v[0, i]
        for off in range(1, n_d):
            total = total + recv_v[off - 1, i].astype(F32)
        own_v[0, i] = total
    dg_out = pltpu.make_async_copy(own_v, dg_hbm, dg_sem)
    dg_out.start()

    def drain(j, carry):
        for copy in outputs(j):
            copy.wait()
        return carry

    lax.fori_loop(0, tiles, drain, 0)
    for c in range(chunks):
        for off in range(1, n_y):
            cross[off, c].wait_send()
            forward[off, c].wait_send()
    to_sibling.wait_send()
    for copy in scatter:
        copy.wait_send()
    dg_out.wait()


def local(n_t, n_d, gate_pre, up_pre, grad_out, down_weight, delta_values, delta_rows, delta_cols, delta_owner):
    tok, ff = gate_pre.shape
    depth = down_weight.shape[1]
    blocks, side = delta_values.shape[0], delta_values.shape[1]
    chunks = 4
    n_y = n_t // CORES
    tiles = ff // widest(ff, TILES)
    smem = pl.BlockSpec(memory_space=pltpu.SMEM)
    anywhere = pl.BlockSpec(memory_space=pl.ANY)
    vmem = pl.BlockSpec(memory_space=pltpu.VMEM)
    dma = pltpu.SemaphoreType.DMA
    return pl.pallas_call(
        functools.partial(kernel, n_t, n_d),
        out_shape=(
            jax.ShapeDtypeStruct((tok, ff), BF16),
            jax.ShapeDtypeStruct((tok, ff), BF16),
            jax.ShapeDtypeStruct((1, CAP, side, side), F32),
        ),
        in_specs=[smem] * 3 + [anywhere] * 4 + [vmem],
        out_specs=(anywhere, anywhere, anywhere),
        scratch_shapes=[
            pltpu.VMEM((tok, ff), BF16),
            pltpu.VMEM((tok, ff), BF16),
            pltpu.VMEM((tok, ff), F32),
            pltpu.VMEM((tok, ff), F32),
            pltpu.VMEM((tok, depth), BF16),
            pltpu.VMEM((ff, depth), BF16),
            pltpu.VMEM((tok, ff), F32),
            pltpu.VMEM((ff // side, tok, side), BF16),
            pltpu.VMEM((depth // side, tok, side), BF16),
            pltpu.VMEM((blocks, side, tok), BF16),
            pltpu.VMEM((blocks + 1, side, side), F32),
            pltpu.VMEM((n_d * CAP, side, side), BF16),
            pltpu.VMEM((n_d - 1, CAP, side, side), BF16),
            pltpu.VMEM((blocks * side, blocks * side), BF16),
            pltpu.VMEM((blocks + 1, tok, side), F32),
            pltpu.VMEM((1, CAP, side, side), F32),
            dma((3,)),
            dma((chunks,)),
            dma((2, tiles)),
            dma,
            dma((2,)),
            dma((n_y - 1, chunks)),
            dma((n_y - 1, chunks)),
            dma((n_y - 1, chunks)),
            dma((n_y - 1, chunks)),
            dma((n_d - 1,)),
            dma((n_d - 1,)),
        ],
        compiler_params=pltpu.CompilerParams(
            collective_id=0, has_side_effects=True, vmem_limit_bytes=56 * 2**20
        ),
    )(delta_rows, delta_cols, delta_owner, gate_pre, up_pre, grad_out, down_weight, delta_values)


def solution(mesh):
    placed = (
        P(("groups", "dp"), "tensor"),
        P(("groups", "dp"), "tensor"),
        P(("groups", "dp", "tensor"), None),
        P("tensor", None),
        P(("groups", "tensor"), None, None),
        P(("groups", "tensor")),
        P(("groups", "tensor")),
        P(("groups", "tensor")),
    )
    return jax.shard_map(
        functools.partial(local, mesh.shape["tensor"], mesh.shape["dp"]),
        mesh=mesh,
        in_specs=placed,
        out_specs=(
            P(("groups", "dp"), "tensor"),
            P(("groups", "dp"), "tensor"),
            P(("groups", "tensor"), "dp", None, None),
        ),
        check_vma=False,
    )
```
